32 devices in a mesh: pts: 16 (over z, y, x), rep: 2 (over core).
Axes of the slice: x: 2, y: 2, z: 4, core: 2. Of those that a mesh axis runs over, the one named last changes fastest.
Arguments:
- points: float32 [3, 65536], P(None, ('pts', 'rep')), may hold values from 0 to 1
- scales: float32 [3], replicated, may hold values from 0.1 to 0.3
- pivots: int32 [4, 128], replicated, may hold values from 0 to 65535, as said below
Outputs:
- factor: float32 [512, 65536], P(None, ('pts', 'rep'))
The draws below stay inside these ranges and needn't reach their ends.
Inputs may be any that keep to these rules, and one draw needn't show every extreme that they name: All 512 indices are distinct. Point i lies on the device whose flat index over pts+rep is i // 2048; no device holds more than 16 pivots of one round, and some device holds exactly 16 in every round.
All inputs are finite; a program needn't handle non-finite values.
Results may differ from the reference program's by a relative error of at most 0.0003.
Values sent between devices are 32-bit elements; how exact they have to be, the bound alone decides.
A program may use at most 64 MiB of HBM per device.

```python
import math
import jax
import jax.numpy as jnp
from jax import lax

DIM = 3
B = 128
R = 4
P_DEV = 2048
NPTS = 65536
CAP = 16


def draw_pivots(key, part):
    device_list = NPTS // P_DEV
    every_slot = device_list * CAP
    order_keys = jax.random.split(jax.random.fold_in(key, 7), device_list)
    orders = jax.vmap(lambda order_key: jax.random.permutation(order_key, P_DEV))(order_keys)
    listed = []
    for round_index in range(R):
        round_seed_key = jax.random.fold_in(key, 100 + round_index)
        heaviest_key, extra_weight_key, jitter_key, permute_key = jax.random.split(round_seed_key, 4)
        heaviest_device = jax.random.randint(heaviest_key, (), 0, device_list)
        extra_weight = jax.random.randint(extra_weight_key, (device_list,), 0, 4)
        extra_weight = jnp.where(jnp.arange(device_list) == heaviest_device, 4, extra_weight)
        jitter_values = jax.random.randint(jitter_key, (every_slot,), 0, 2 ** 18)
        slot_owner_device = jnp.arange(every_slot) // CAP
        device_scores = (jitter_values + extra_weight[slot_owner_device] * 2 ** 18) * every_slot + jnp.arange(every_slot)
        unused, picked = lax.top_k(device_scores, B)
        device_of = picked // CAP
        slot_of = picked % CAP
        local_index = orders[device_of, round_index * CAP + slot_of]
        indices = device_of * P_DEV + local_index
        listed.append(jax.random.permutation(permute_key, indices))
    return jnp.stack(listed).astype(jnp.int32)


def shard_levels(own_key, dims, cuts, smallest, high):
    def one(axis_at, parts):
        draws = jax.random.uniform(jax.random.fold_in(jax.random.fold_in(own_key, 6), axis_at), (parts,), jnp.float32, smallest / len(cuts), high / len(cuts))
        return jnp.repeat(jnp.exp(draws), dims[axis_at] // parts).reshape((-1,) + (1,) * (len(dims) - axis_at - 1))

    level = one(*cuts[0])
    for cut in cuts[1:]:
        level = level * one(*cut)
    return level


def setup_inputs(seed: int = 0) -> dict:
    keys = jax.random.split(jax.random.key(seed), 4)
    return {
        "points": jnp.clip(1.0 * jax.random.uniform(keys[0], (DIM, NPTS), jnp.float32) ** shard_levels(keys[0], (DIM, NPTS), ((1, 32),), -0.2, 0.2), 0.0, 1.0),
        "scales": jnp.clip(jnp.exp(jax.random.uniform(keys[1], (DIM,), jnp.float32, math.log(0.1), math.log(0.3))), 0.1, 0.3),
        "pivots": draw_pivots(jax.random.fold_in(keys[3], 71), 0),
    }


nugget_level = 0.1

def kernel_block(anchors, targets, inverse):
    squared = jnp.zeros((anchors.shape[1], targets.shape[1]), jnp.float32)
    for component in range(anchors.shape[0]):
        offset = (anchors[component][:, None] - targets[component][None, :]) * inverse[component]
        squared = squared + offset * offset
    return jnp.exp(-0.5 * squared)

def reference(points, scales, pivots):
    inverse = 1.0 / scales
    identity = jnp.eye(B, dtype=jnp.float32)
    blocks = []
    for round_index in range(R):
        chosen = pivots[round_index]
        anchors = points[:, chosen]
        residual = kernel_block(anchors, anchors, inverse) + nugget_level * identity
        columns = kernel_block(anchors, points, inverse)
        for earlier in blocks:
            earlier_rows = earlier[:, chosen]
            residual = residual - jnp.dot(earlier_rows.T, earlier_rows, precision=lax.Precision.HIGHEST)
            columns = columns - jnp.dot(earlier_rows.T, earlier, precision=lax.Precision.HIGHEST)
        factor = jnp.linalg.cholesky(residual)
        blocks.append(lax.linalg.triangular_solve(factor, columns, left_side=True, lower=True))
    return jnp.concatenate(blocks, axis=0)
```

```python
import functools
import math

import jax
import jax.numpy as jnp
from jax import lax
from jax.experimental import pallas as pl
from jax.experimental.pallas import tpu as pltpu
from jax.sharding import PartitionSpec as P

nugget_level = 0.1
HIGHEST = lax.Precision.HIGHEST
LANES = 128
GROUP = 8


def split_three(value):
    high = value.astype(jnp.bfloat16)
    rest = value - high.astype(jnp.float32)
    middle = rest.astype(jnp.bfloat16)
    low = (rest - middle.astype(jnp.float32)).astype(jnp.bfloat16)
    return high, middle, low


def exchange_kernel(
    mesh_shape, points_ref, pivots_ref, out_ref, table, mine, landed, send_sem, recv_sem
):
    pts_count, rep_count = mesh_shape
    devices = pts_count * rep_count
    here = lax.axis_index("pts") * rep_count + lax.axis_index("rep")
    dims, point_count = points_ref.shape
    rounds, pivot_count = pivots_ref.shape

    def place(step):
        peer = lax.rem(here + step, devices)
        return {"pts": peer // rep_count, "rep": lax.rem(peer, rep_count)}, peer

    barrier = pltpu.get_barrier_semaphore()

    def greet(step, carry):
        target, _ = place(step)
        pl.semaphore_signal(
            barrier, inc=1, device_id=target, device_id_type=pl.DeviceIdType.MESH
        )
        return carry

    lax.fori_loop(1, devices, greet, 0)

    chunks = point_count // LANES
    table[...] = jnp.zeros_like(table)
    for chunk in range(chunks):
        table[chunk * GROUP:chunk * GROUP + dims, :] = points_ref[
            :, chunk * LANES:(chunk + 1) * LANES
        ]
    pieces = split_three(table[...])
    lane_of = lax.broadcasted_iota(jnp.int32, (LANES, pivot_count), 0)
    for round_index in range(rounds):
        local = pivots_ref[round_index:round_index + 1, :] - here * point_count
        owned = (local >= 0) & (local < point_count)
        local = jnp.where(owned, local, 0)
        low = lax.rem(local, LANES)
        high = jnp.where(owned, local // LANES, -1)
        picks = (lane_of == low).astype(jnp.bfloat16)
        found = sum(
            jnp.dot(piece, picks, preferred_element_type=jnp.float32) for piece in pieces
        )
        total = jnp.zeros((GROUP, pivot_count), jnp.float32)
        for chunk in range(chunks):
            total = total + jnp.where(
                high == chunk, found[chunk * GROUP:(chunk + 1) * GROUP, :], 0.0
            )
        mine[:, round_index * pivot_count:(round_index + 1) * pivot_count] = total[:dims]

    pl.semaphore_wait(barrier, devices - 1)

    def copy_to(step):
        target, peer = place(step)
        return pltpu.make_async_remote_copy(
            src_ref=mine,
            dst_ref=landed.at[here],
            send_sem=send_sem.at[peer],
            recv_sem=recv_sem.at[here],
            device_id=target,
            device_id_type=pl.DeviceIdType.MESH,
        )

    def copy_from(step):
        _, peer = place(step)
        return pltpu.make_async_remote_copy(
            src_ref=mine,
            dst_ref=landed.at[peer],
            send_sem=send_sem.at[peer],
            recv_sem=recv_sem.at[peer],
            device_id=place(step)[0],
            device_id_type=pl.DeviceIdType.MESH,
        )

    def send(step, carry):
        copy_to(step).start()
        return carry

    def receive(step, total):
        copy_from(step).wait_recv()
        return total + landed[place(step)[1]]

    def finish(step, carry):
        copy_from(step).wait_send()
        return carry

    lax.fori_loop(1, devices, send, 0)
    total = lax.fori_loop(1, devices, receive, mine[...])
    out_ref[...] = jnp.zeros_like(out_ref)
    out_ref[:dims, :] = total
    lax.fori_loop(1, devices, finish, 0)


def reciprocal(value):
    rough = pl.reciprocal(value, approx=True)
    rough = rough * (2.0 - value * rough)
    return rough * (2.0 - value * rough)


def spread_lane(block, lane):
    return jnp.broadcast_to(block[:, lane:lane + 1], block.shape)


def spread_row(block, row):
    return jnp.broadcast_to(block[row:row + 1, :], block.shape)


def invert_factor(block):
    size = block.shape[0]
    count = size // GROUP
    row_of = lax.broadcasted_iota(jnp.int32, (GROUP, size), 0)
    lane_of = lax.broadcasted_iota(jnp.int32, (GROUP, size), 1)
    left = [block[GROUP * index:GROUP * (index + 1), :] for index in range(count)]
    right = [
        jnp.where(row_of + GROUP * index == lane_of, 1.0, 0.0) for index in range(count)
    ]
    result = []
    for panel in range(count):
        base = GROUP * panel
        spread = [spread_lane(left[panel], base + column) for column in range(GROUP)]
        s = {
            (i, j): spread_row(spread[j], i) for j in range(GROUP) for i in range(j, GROUP)
        }
        y_left = [spread_row(left[panel], row) for row in range(GROUP)]
        y_right = [spread_row(right[panel], row) for row in range(GROUP)]
        inverse = [None] * GROUP
        factor = {}
        for first in range(0, GROUP, 2):
            second = first + 1
            a, b, c = s[first, first], s[second, first], s[second, second]
            det = a * c - b * b
            inverse[first] = reciprocal(a)
            inverse[second] = a * reciprocal(det)
            for column in (first, second):
                for i in range(column + 1, GROUP):
                    factor[i, column] = s[i, column] * inverse[column]
                for j in range(column + 1, GROUP):
                    for i in range(j, GROUP):
                        if (i, j) == (second, second):
                            continue
                        s[i, j] = s[i, j] - factor[j, column] * s[i, column]
                for i in range(column + 1, GROUP):
                    y_left[i] = y_left[i] - factor[i, column] * y_left[column]
                    y_right[i] = y_right[i] - factor[i, column] * y_right[column]
        rows = jnp.zeros((GROUP, size), jnp.float32)
        roots = jnp.zeros((GROUP, size), jnp.float32)
        for row in range(GROUP):
            rows = jnp.where(row_of == row, y_right[row], rows)
            roots = jnp.where(row_of == row, inverse[row], roots)
        result.append(rows * jnp.sqrt(roots))
        if panel == count - 1:
            break
        w_left = [y_left[row] * inverse[row] for row in range(GROUP)]
        w_right = [y_right[row] * inverse[row] for row in range(GROUP)]
        for column in reversed(range(GROUP)):
            for row in range(column):
                w_left[row] = w_left[row] - factor[column, row] * w_left[column]
                w_right[row] = w_right[row] - factor[column, row] * w_right[column]
        for later in range(panel + 1, count):
            weights = [spread_lane(left[later], base + column) for column in range(GROUP)]
            for column in range(GROUP):
                left[later] = left[later] - weights[column] * w_left[column]
                right[later] = right[later] - weights[column] * w_right[column]
    return jnp.concatenate(result, axis=0)


def factor_kernel(
    rounds, points_ref, scales_ref, anchors_ref, out_ref, table, anchor_wide, rows_ref, held, sems
):
    dims, point_count = points_ref.shape
    total = anchors_ref.shape[1]
    pivot_count = total // rounds
    tile = 512
    tiles = point_count // tile
    constant = math.sqrt(0.5 * math.log2(math.e))
    weights = [
        constant / jnp.full((1, LANES), scales_ref[axis], jnp.float32) for axis in range(dims)
    ]
    upright = jnp.transpose(anchors_ref[...])
    for axis in range(dims):
        anchor_wide[axis] = upright[:, axis:axis + 1] * weights[axis]
        rows_ref[axis:axis + 1, :] = anchors_ref[axis:axis + 1, :] * jnp.concatenate(
            [weights[axis]] * (total // LANES), axis=1
        )

    def covariance(start, count, targets):
        pieces = []
        for column in range(targets[0].shape[1] // LANES):
            squared = None
            for axis in range(dims):
                offset = anchor_wide[axis, pl.ds(start, count), :] - targets[axis][
                    :, column * LANES:(column + 1) * LANES
                ]
                square = offset * offset
                squared = square if squared is None else squared + square
            pieces.append(jnp.exp2(-squared))
        return jnp.concatenate(pieces, axis=1)

    def one_round(round_index, carry):
        start = pl.multiple_of(round_index * pivot_count, pivot_count)
        here = pl.ds(start, pivot_count)
        unit = jnp.where(
            lax.broadcasted_iota(jnp.int32, (pivot_count, total), 0) + start
            == lax.broadcasted_iota(jnp.int32, (pivot_count, total), 1),
            1.0,
            0.0,
        )
        own = covariance(
            start, pivot_count, [rows_ref[axis:axis + 1, :] for axis in range(dims)]
        )
        table[here, :] = jnp.concatenate([own + nugget_level * unit, unit], axis=1)

        def subtract(earlier, inner):
            seen = pl.ds(pl.multiple_of(earlier * pivot_count, pivot_count), pivot_count)
            table[here, :] = table[here, :] - lax.dot_general(
                table[seen, here],
                table[seen, :],
                (((0,), (0,)), ((), ())),
                precision=HIGHEST,
                preferred_element_type=jnp.float32,
            )
            return inner

        lax.fori_loop(0, round_index, subtract, 0)
        inverse = invert_factor(table[here, here])
        table[here, :] = jnp.dot(
            inverse, table[here, :], precision=HIGHEST, preferred_element_type=jnp.float32
        )
        return carry

    lax.fori_loop(0, rounds, one_round, 0)

    def copy_out(index):
        span = pl.ds(pl.multiple_of(index * tile, tile), tile)
        return pltpu.make_async_copy(held.at[:, span], out_ref.at[:, span], sems.at[index])

    def one_tile(index, carry):
        span = pl.ds(pl.multiple_of(index * tile, tile), tile)
        targets = [
            points_ref[axis:axis + 1, span]
            * jnp.concatenate([weights[axis]] * (tile // LANES), axis=1)
            for axis in range(dims)
        ]
        block = covariance(0, total, targets)
        for round_index in range(rounds):
            low, high = round_index * pivot_count, (round_index + 1) * pivot_count
            held[low:high, span] = jnp.dot(
                table[low:high, total:total + high],
                block[:high],
                precision=HIGHEST,
                preferred_element_type=jnp.float32,
            )
        copy_out(index).start()
        return carry

    lax.fori_loop(0, tiles, one_tile, 0)

    def finish(index, carry):
        copy_out(index).wait()
        return carry

    lax.fori_loop(0, tiles, finish, 0)


def per_device(mesh_shape, points, scales, pivots):
    dims, point_count = points.shape
    rounds, pivot_count = pivots.shape
    total = rounds * pivot_count
    devices = mesh_shape[0] * mesh_shape[1]
    vmem = pl.BlockSpec(memory_space=pltpu.VMEM)
    anchors = pl.pallas_call(
        functools.partial(exchange_kernel, mesh_shape),
        out_shape=jax.ShapeDtypeStruct((GROUP, total), jnp.float32),
        in_specs=[vmem, vmem],
        out_specs=vmem,
        scratch_shapes=[
            pltpu.VMEM((point_count // LANES * GROUP, LANES), jnp.float32),
            pltpu.VMEM((dims, total), jnp.float32),
            pltpu.VMEM((devices, dims, total), jnp.float32),
            pltpu.SemaphoreType.DMA((devices,)),
            pltpu.SemaphoreType.DMA((devices,)),
        ],
        compiler_params=pltpu.CompilerParams(
            collective_id=0, has_side_effects=True, vmem_limit_bytes=32 * 2 ** 20
        ),
        name="exchange_anchors",
    )(points, pivots)
    return pl.pallas_call(
        functools.partial(factor_kernel, rounds),
        out_shape=jax.ShapeDtypeStruct((total, point_count), jnp.float32),
        in_specs=[vmem, pl.BlockSpec(memory_space=pltpu.SMEM), vmem],
        out_specs=pl.BlockSpec(memory_space=pl.ANY),
        scratch_shapes=[
            pltpu.VMEM((total, 2 * total), jnp.float32),
            pltpu.VMEM((dims, total, LANES), jnp.float32),
            pltpu.VMEM((GROUP, total), jnp.float32),
            pltpu.VMEM((total, point_count), jnp.float32),
            pltpu.SemaphoreType.DMA((point_count // 512,)),
        ],
        compiler_params=pltpu.CompilerParams(vmem_limit_bytes=48 * 2 ** 20),
        name="factor_columns",
    )(points, scales, anchors)


def solution(mesh):
    placed = (P(None, ("pts", "rep")), P(), P())
    mesh_shape = (mesh.shape["pts"], mesh.shape["rep"])
    return jax.shard_map(
        functools.partial(per_device, mesh_shape),
        mesh=mesh,
        in_specs=placed,
        out_specs=P(None, ("pts", "rep")),
        check_vma=False,
    )
```

```python
import functools
import math

import jax
import jax.numpy as jnp
from jax import lax
from jax.experimental import pallas as pl
from jax.experimental.pallas import tpu as pltpu
from jax.sharding import PartitionSpec as P

nugget_level = 0.1
HIGHEST = lax.Precision.HIGHEST
LANES = 128
GROUP = 8


def split_three(value):
    high = value.astype(jnp.bfloat16)
    rest = value - high.astype(jnp.float32)
    middle = rest.astype(jnp.bfloat16)
    low = (rest - middle.astype(jnp.float32)).astype(jnp.bfloat16)
    return high, middle, low


def exchange_kernel(
    mesh_shape,
    inner,
    points_hbm,
    scales_hbm,
    pivots_hbm,
    out_ref,
    points_ref,
    scales_ref,
    pivots_ref,
    table,
    mine,
    pair_sum,
    landed_near,
    landed_far,
    load_sems,
    near_send,
    near_recv,
    far_send,
    far_recv,
):
    pts_count, rep_count = mesh_shape
    devices = pts_count * rep_count
    here = lax.axis_index("pts") * rep_count + lax.axis_index("rep")
    dims, point_count = points_ref.shape
    rounds, pivot_count = pivots_ref.shape
    within = lax.rem(here, inner)

    def place(peer):
        return {"pts": peer // rep_count, "rep": lax.rem(peer, rep_count)}

    near = [place(here - within + lax.rem(within + step, inner)) for step in range(1, inner)]
    far = [place(lax.rem(here + step * inner, devices)) for step in range(1, devices // inner)]

    loads = [
        pltpu.make_async_copy(points_hbm, points_ref, load_sems.at[0]),
        pltpu.make_async_copy(pivots_hbm, pivots_ref, load_sems.at[1]),
        pltpu.make_async_copy(scales_hbm, scales_ref, load_sems.at[2]),
    ]
    for load in loads:
        load.start()

    barrier = pltpu.get_barrier_semaphore()
    for target in near + far:
        pl.semaphore_signal(
            barrier, inc=1, device_id=target, device_id_type=pl.DeviceIdType.MESH
        )

    chunks = point_count // LANES
    table[...] = jnp.zeros_like(table)
    for load in loads:
        load.wait()
    for chunk in range(chunks):
        table[chunk * GROUP:chunk * GROUP + dims, :] = points_ref[
            :, chunk * LANES:(chunk + 1) * LANES
        ]
    pieces = split_three(table[...])
    lane_of = lax.broadcasted_iota(jnp.int32, (LANES, pivot_count), 0)
    for round_index in range(rounds):
        local = pivots_ref[round_index:round_index + 1, :] - here * point_count
        owned = (local >= 0) & (local < point_count)
        local = jnp.where(owned, local, 0)
        low = lax.rem(local, LANES)
        high = jnp.where(owned, local // LANES, -1)
        picks = (lane_of == low).astype(jnp.bfloat16)
        found = sum(
            jnp.dot(piece, picks, preferred_element_type=jnp.float32) for piece in pieces
        )
        total = jnp.zeros((GROUP, pivot_count), jnp.float32)
        for chunk in range(chunks):
            total = total + jnp.where(
                high == chunk, found[chunk * GROUP:(chunk + 1) * GROUP, :], 0.0
            )
        mine[:, round_index * pivot_count:(round_index + 1) * pivot_count] = total[:dims]

    pl.semaphore_wait(barrier, len(near) + len(far))

    def exchange(source, landed, targets, send_sems, recv_sems):
        copies = [
            pltpu.make_async_remote_copy(
                src_ref=source,
                dst_ref=landed.at[index],
                send_sem=send_sems.at[index],
                recv_sem=recv_sems.at[index],
                device_id=target,
                device_id_type=pl.DeviceIdType.MESH,
            )
            for index, target in enumerate(targets)
        ]
        for copy in copies:
            copy.start()
        total = source[...]
        for index, copy in enumerate(copies):
            copy.wait_recv()
            total = total + landed[index]
        return total, copies

    total, near_copies = exchange(mine, landed_near, near, near_send, near_recv)
    pair_sum[...] = total
    total, far_copies = exchange(pair_sum, landed_far, far, far_send, far_recv)
    constant = math.sqrt(0.5 * math.log2(math.e))
    out_ref[...] = jnp.zeros_like(out_ref)
    for axis in range(dims):
        weight = constant / jnp.full((1, total.shape[1]), scales_ref[axis], jnp.float32)
        out_ref[axis:axis + 1, :] = total[axis:axis + 1, :] * weight
        out_ref[dims + axis:dims + axis + 1, :] = weight
    for copy in near_copies + far_copies:
        copy.wait_send()


def reciprocal(value):
    return pl.reciprocal(value, approx=True)


def spread_lane(block, lane):
    return jnp.broadcast_to(block[:, lane:lane + 1], block.shape)


def spread_row(block, row):
    return jnp.broadcast_to(block[row:row + 1, :], block.shape)


def invert_factor(block, beside):
    size = block.shape[0]
    count = size // GROUP
    row_of = lax.broadcasted_iota(jnp.int32, (GROUP, size), 0)
    lane_of = lax.broadcasted_iota(jnp.int32, (GROUP, size), 1)
    left = [block[GROUP * index:GROUP * (index + 1), :] for index in range(count)]
    right = [
        jnp.where(row_of + GROUP * index == lane_of, 1.0, 0.0) for index in range(count)
    ]
    result = []
    for panel in range(count):
        base = GROUP * panel
        beside(panel, count)
        spread = [spread_lane(left[panel], base + column) for column in range(GROUP)]
        s = {
            (i, j): spread_row(spread[j], i) for j in range(GROUP) for i in range(j, GROUP)
        }
        y_left = [spread_row(left[panel], row) for row in range(GROUP)]
        y_right = [spread_row(right[panel], row) for row in range(GROUP)]
        inverse = [None] * GROUP
        factor = {}
        for first in range(0, GROUP, 2):
            second = first + 1
            a, b, c = s[first, first], s[second, first], s[second, second]
            det = a * c - b * b
            inverse[first] = reciprocal(a)
            inverse[second] = a * reciprocal(det)
            for column in (first, second):
                for i in range(column + 1, GROUP):
                    factor[i, column] = s[i, column] * inverse[column]
                for j in range(column + 1, GROUP):
                    for i in range(j, GROUP):
                        if (i, j) == (second, second):
                            continue
                        s[i, j] = s[i, j] - factor[j, column] * s[i, column]
                for i in range(column + 1, GROUP):
                    y_left[i] = y_left[i] - factor[i, column] * y_left[column]
                    y_right[i] = y_right[i] - factor[i, column] * y_right[column]
        rows = jnp.zeros((GROUP, size), jnp.float32)
        roots = jnp.zeros((GROUP, size), jnp.float32)
        for row in range(GROUP):
            rows = jnp.where(row_of == row, y_right[row], rows)
            roots = jnp.where(row_of == row, inverse[row], roots)
        result.append(rows * jnp.sqrt(roots))
        if panel == count - 1:
            break
        w_left = [y_left[row] * inverse[row] for row in range(GROUP)]
        w_right = [y_right[row] * inverse[row] for row in range(GROUP)]
        for column in reversed(range(GROUP)):
            for row in range(column):
                w_left[row] = w_left[row] - factor[column, row] * w_left[column]
                w_right[row] = w_right[row] - factor[column, row] * w_right[column]
        for later in range(panel + 1, count):
            weights = [spread_lane(left[later], base + column) for column in range(GROUP)]
            for column in range(GROUP):
                left[later] = left[later] - weights[column] * w_left[column]
                right[later] = right[later] - weights[column] * w_right[column]
    return jnp.concatenate(result, axis=0)


def factor_kernel(
    rounds,
    points_hbm,
    anchors_ref,
    out_ref,
    points_ref,
    table,
    anchor_wide,
    inverse_high,
    inverse_low,
    block_high,
    block_low,
    held,
    load_sem,
    sems,
):
    dims, point_count = points_ref.shape
    total = anchors_ref.shape[1]
    pivot_count = total // rounds
    tile = point_count // rounds
    load = pltpu.make_async_copy(points_hbm, points_ref, load_sem)
    load.start()
    weights = [anchors_ref[dims + axis:dims + axis + 1, :LANES] for axis in range(dims)]
    upright = jnp.transpose(anchors_ref[...])
    for axis in range(dims):
        anchor_wide[axis] = jnp.broadcast_to(upright[:, axis:axis + 1], (total, LANES))
    load.wait()

    def covariance(start, count, targets):
        pieces = []
        for column in range(targets[0].shape[1] // LANES):
            squared = None
            for axis in range(dims):
                offset = anchor_wide[axis, pl.ds(start, count), :] - targets[axis][
                    :, column * LANES:(column + 1) * LANES
                ]
                square = offset * offset
                squared = square if squared is None else squared + square
            pieces.append(jnp.exp2(-squared))
        return jnp.concatenate(pieces, axis=1)

    def one_round(round_index, carry):
        start = pl.multiple_of(round_index * pivot_count, pivot_count)
        here = pl.ds(start, pivot_count)
        span = pl.ds(pl.multiple_of(round_index * tile, tile), tile)
        lane_of = lax.broadcasted_iota(jnp.int32, (pivot_count, total), 1)
        row_of = lax.broadcasted_iota(jnp.int32, (pivot_count, total), 0) + start
        own = covariance(
            start, pivot_count, [anchors_ref[axis:axis + 1, :] for axis in range(dims)]
        )
        own = own + jnp.where(row_of == lane_of, nugget_level, 0.0)
        table[here, :] = jnp.where(lane_of >= start, own, 0.0)

        def subtract(earlier, inner):
            before = pl.multiple_of(earlier * pivot_count, pivot_count)
            seen = pl.ds(before, pivot_count)
            kept = (lane_of < before + pivot_count) | (lane_of >= start)
            table[here, :] = table[here, :] - lax.dot_general(
                table[seen, here],
                jnp.where(kept, table[seen, :], 0.0),
                (((0,), (0,)), ((), ())),
                precision=HIGHEST,
                preferred_element_type=jnp.float32,
            )
            return inner

        lax.fori_loop(0, round_index, subtract, 0)

        targets = [
            points_ref[axis:axis + 1, span]
            * jnp.concatenate([weights[axis]] * (tile // LANES), axis=1)
            for axis in range(dims)
        ]

        def beside(step, steps):
            size = total // steps
            part = slice(step * size, (step + 1) * size)
            values = covariance(step * size, size, targets)
            high = values.astype(jnp.bfloat16)
            block_high[part, span] = high
            block_low[part, span] = (values - high.astype(jnp.float32)).astype(jnp.bfloat16)

        inverse = invert_factor(table[here, here], beside)
        table[here, :] = jnp.dot(
            inverse, table[here, :], precision=HIGHEST, preferred_element_type=jnp.float32
        )
        table[here, here] = inverse
        final = jnp.where(lane_of < start + pivot_count, table[here, :], 0.0)
        high = final.astype(jnp.bfloat16)
        inverse_high[here, :] = high
        inverse_low[here, :] = (final - high.astype(jnp.float32)).astype(jnp.bfloat16)
        return carry

    lax.fori_loop(0, rounds, one_round, 0)

    half = total // 2

    def copy_out(index):
        span = pl.ds(pl.multiple_of(index * tile, tile), tile)
        return pltpu.make_async_copy(held.at[:, span], out_ref.at[:, span], sems.at[index])

    def product(rows, depth, span):
        def multiply(a, b):
            return jnp.dot(
                a[rows, depth], b[depth, span], preferred_element_type=jnp.float32
            )

        return (
            multiply(inverse_high, block_low) + multiply(inverse_low, block_high)
        ) + multiply(inverse_high, block_high)

    def one_tile(index, carry):
        span = pl.ds(pl.multiple_of(index * tile, tile), tile)
        top, bottom = slice(0, half), slice(half, total)
        held[:, span] = product(slice(0, total), top, span)
        held[bottom, span] = held[bottom, span] + product(bottom, bottom, span)
        copy_out(index).start()
        return carry

    lax.fori_loop(0, rounds, one_tile, 0)

    def finish(index, carry):
        copy_out(index).wait()
        return carry

    lax.fori_loop(0, rounds, finish, 0)


def per_device(mesh_shape, points, scales, pivots):
    dims, point_count = points.shape
    rounds, pivot_count = pivots.shape
    total = rounds * pivot_count
    devices = mesh_shape[0] * mesh_shape[1]
    inner = 1
    while inner * inner < devices:
        inner *= 2
    if devices % inner:
        inner = devices
    near, far = inner - 1, devices // inner - 1
    vmem = pl.BlockSpec(memory_space=pltpu.VMEM)
    anywhere = pl.BlockSpec(memory_space=pl.ANY)
    anchors = pl.pallas_call(
        functools.partial(exchange_kernel, mesh_shape, inner),
        out_shape=jax.ShapeDtypeStruct((GROUP, total), jnp.float32),
        in_specs=[anywhere] * 3,
        out_specs=vmem,
        scratch_shapes=[
            pltpu.VMEM((dims, point_count), jnp.float32),
            pltpu.SMEM((dims,), jnp.float32),
            pltpu.VMEM((rounds, pivot_count), jnp.int32),
            pltpu.VMEM((point_count // LANES * GROUP, LANES), jnp.float32),
            pltpu.VMEM((dims, total), jnp.float32),
            pltpu.VMEM((dims, total), jnp.float32),
            pltpu.VMEM((max(near, 1), dims, total), jnp.float32),
            pltpu.VMEM((max(far, 1), dims, total), jnp.float32),
            pltpu.SemaphoreType.DMA((3,)),
            pltpu.SemaphoreType.DMA((max(near, 1),)),
            pltpu.SemaphoreType.DMA((max(near, 1),)),
            pltpu.SemaphoreType.DMA((max(far, 1),)),
            pltpu.SemaphoreType.DMA((max(far, 1),)),
        ],
        compiler_params=pltpu.CompilerParams(
            collective_id=0, has_side_effects=True, vmem_limit_bytes=56 * 2 ** 20
        ),
        name="exchange_anchors",
    )(points, scales, pivots)
    return pl.pallas_call(
        functools.partial(factor_kernel, rounds),
        out_shape=jax.ShapeDtypeStruct((total, point_count), jnp.float32),
        in_specs=[anywhere, vmem],
        out_specs=anywhere,
        scratch_shapes=[
            pltpu.VMEM((dims, point_count), jnp.float32),
            pltpu.VMEM((total, total), jnp.float32),
            pltpu.VMEM((dims, total, LANES), jnp.float32),
            pltpu.VMEM((total, total), jnp.bfloat16),
            pltpu.VMEM((total, total), jnp.bfloat16),
            pltpu.VMEM((total, point_count), jnp.bfloat16),
            pltpu.VMEM((total, point_count), jnp.bfloat16),
            pltpu.VMEM((total, point_count), jnp.float32),
            pltpu.SemaphoreType.DMA,
            pltpu.SemaphoreType.DMA((rounds,)),
        ],
        compiler_params=pltpu.CompilerParams(vmem_limit_bytes=56 * 2 ** 20),
        name="factor_columns",
    )(points, anchors)


def solution(mesh):
    placed = (P(None, ("pts", "rep")), P(), P())
    mesh_shape = (mesh.shape["pts"], mesh.shape["rep"])
    return jax.shard_map(
        functools.partial(per_device, mesh_shape),
        mesh=mesh,
        in_specs=placed,
        out_specs=P(None, ("pts", "rep")),
        check_vma=False,
    )
```

```python
import functools
import math

import jax
import jax.numpy as jnp
from jax import lax
from jax.experimental import pallas as pl
from jax.experimental.pallas import tpu as pltpu
from jax.sharding import PartitionSpec as P

nugget_level = 0.1
HIGHEST = lax.Precision.HIGHEST
LANES = 128
GROUP = 8


def split_three(value):
    high = value.astype(jnp.bfloat16)
    rest = value - high.astype(jnp.float32)
    middle = rest.astype(jnp.bfloat16)
    low = (rest - middle.astype(jnp.float32)).astype(jnp.bfloat16)
    return high, middle, low


def exchange_kernel(
    mesh_shape,
    inner,
    points_hbm,
    scales_hbm,
    pivots_hbm,
    out_ref,
    points_ref,
    scales_ref,
    pivots_ref,
    table,
    mine,
    pair_sum,
    landed_near,
    landed_far,
    load_sems,
    near_send,
    near_recv,
    far_send,
    far_recv,
):
    pts_count, rep_count = mesh_shape
    devices = pts_count * rep_count
    here = lax.axis_index("pts") * rep_count + lax.axis_index("rep")
    dims, point_count = points_ref.shape
    rounds, pivot_count = pivots_ref.shape
    within = lax.rem(here, inner)

    def place(peer):
        return {"pts": peer // rep_count, "rep": lax.rem(peer, rep_count)}

    near = [place(here - within + lax.rem(within + step, inner)) for step in range(1, inner)]
    far = [place(lax.rem(here + step * inner, devices)) for step in range(1, devices // inner)]

    loads = [
        pltpu.make_async_copy(points_hbm, points_ref, load_sems.at[0]),
        pltpu.make_async_copy(pivots_hbm, pivots_ref, load_sems.at[1]),
        pltpu.make_async_copy(scales_hbm, scales_ref, load_sems.at[2]),
    ]
    for load in loads:
        load.start()

    barrier = pltpu.get_barrier_semaphore()
    for target in near + far:
        pl.semaphore_signal(
            barrier, inc=1, device_id=target, device_id_type=pl.DeviceIdType.MESH
        )

    chunks = point_count // LANES
    table[...] = jnp.zeros_like(table)
    for load in loads:
        load.wait()
    for chunk in range(chunks):
        table[chunk * GROUP:chunk * GROUP + dims, :] = points_ref[
            :, chunk * LANES:(chunk + 1) * LANES
        ]
    pieces = split_three(table[...])
    lane_of = lax.broadcasted_iota(jnp.int32, (LANES, pivot_count), 0)
    for round_index in range(rounds):
        local = pivots_ref[round_index:round_index + 1, :] - here * point_count
        owned = (local >= 0) & (local < point_count)
        local = jnp.where(owned, local, 0)
        low = lax.rem(local, LANES)
        high = jnp.where(owned, local // LANES, -1)
        picks = (lane_of == low).astype(jnp.bfloat16)
        found = sum(
            jnp.dot(piece, picks, preferred_element_type=jnp.float32) for piece in pieces
        )
        total = jnp.zeros((GROUP, pivot_count), jnp.float32)
        for chunk in range(chunks):
            total = total + jnp.where(
                high == chunk, found[chunk * GROUP:(chunk + 1) * GROUP, :], 0.0
            )
        mine[:, round_index * pivot_count:(round_index + 1) * pivot_count] = total[:dims]

    pl.semaphore_wait(barrier, len(near) + len(far))

    def exchange(source, landed, targets, send_sems, recv_sems):
        copies = [
            pltpu.make_async_remote_copy(
                src_ref=source,
                dst_ref=landed.at[index],
                send_sem=send_sems.at[index],
                recv_sem=recv_sems.at[index],
                device_id=target,
                device_id_type=pl.DeviceIdType.MESH,
            )
            for index, target in enumerate(targets)
        ]
        for copy in copies:
            copy.start()
        total = source[...]
        for index, copy in enumerate(copies):
            copy.wait_recv()
            total = total + landed[index]
        return total, copies

    total, near_copies = exchange(mine, landed_near, near, near_send, near_recv)
    pair_sum[...] = total
    total, far_copies = exchange(pair_sum, landed_far, far, far_send, far_recv)
    constant = math.sqrt(0.5 * math.log2(math.e))
    out_ref[...] = jnp.zeros_like(out_ref)
    for axis in range(dims):
        weight = constant / jnp.full((1, total.shape[1]), scales_ref[axis], jnp.float32)
        out_ref[axis:axis + 1, :] = total[axis:axis + 1, :] * weight
        out_ref[dims + axis:dims + axis + 1, :] = weight
    for copy in near_copies + far_copies:
        copy.wait_send()


def reciprocal(value):
    return pl.reciprocal(value, approx=True)


def spread_lane(block, lane):
    return jnp.broadcast_to(block[:, lane:lane + 1], block.shape)


def spread_row(block, row):
    return jnp.broadcast_to(block[row:row + 1, :], block.shape)


def invert_factor(block, beside):
    size = block.shape[0]
    count = size // GROUP
    row_of = lax.broadcasted_iota(jnp.int32, (GROUP, size), 0)
    lane_of = lax.broadcasted_iota(jnp.int32, (GROUP, size), 1)
    state = [block[GROUP * index:GROUP * (index + 1), :] for index in range(count)]
    result = []
    for panel in range(count):
        base = GROUP * panel
        beside(panel, count)
        inside = (lane_of >= base) & (lane_of < base + GROUP)
        unit = jnp.where(row_of + base == lane_of, 1.0, 0.0)
        spread = [spread_lane(state[panel], base + column) for column in range(GROUP)]
        s = {
            (i, j): spread_row(spread[j], i) for j in range(GROUP) for i in range(j, GROUP)
        }
        own = jnp.where(inside, unit, state[panel])
        y = [spread_row(own, row) for row in range(GROUP)]
        more = panel + 1 < count
        if more:
            beyond = [
                spread_lane(state[panel + 1], base + column) for column in range(GROUP)
            ]
            follower = jnp.where(inside, 0.0, state[panel + 1])
        inverse = [None] * GROUP
        factor = {}
        z = [None] * GROUP
        for first in range(0, GROUP, 2):
            second = first + 1
            a, b, c = s[first, first], s[second, first], s[second, second]
            over = reciprocal(a * c - b * b)
            inverse[first] = reciprocal(a)
            inverse[second] = a * over
            urgent = {
                (i, j)
                for j in range(second + 1, min(second + 3, GROUP))
                for i in range(j, min(second + 3, GROUP))
            }
            for column in (first, second):
                for i in range(column + 1, GROUP):
                    factor[i, column] = s[i, column] * inverse[column]
                for j in range(column + 1, GROUP):
                    for i in range(j, GROUP):
                        if (i, j) == (second, second):
                            continue
                        if column == second and (i, j) in urgent:
                            change = (s[i, column] * s[j, column]) * a * over
                        else:
                            change = factor[j, column] * s[i, column]
                        s[i, j] = s[i, j] - change
                for i in range(column + 1, GROUP):
                    y[i] = y[i] - factor[i, column] * y[column]
                z[column] = y[column] * inverse[column]
                if more:
                    for k in range(column + 1, GROUP):
                        beyond[k] = beyond[k] - beyond[column] * factor[k, column]
                    follower = follower - beyond[column] * z[column]
        rows, roots = y[0], inverse[0]
        for row in range(1, GROUP):
            rows = jnp.where(row_of == row, y[row], rows)
            roots = jnp.where(row_of == row, inverse[row], roots)
        result.append(jnp.where(lane_of < base + GROUP, rows * jnp.sqrt(roots), 0.0))
        if not more:
            break
        state[panel + 1] = follower
        if panel + 2 == count:
            continue
        for column in reversed(range(GROUP)):
            for row in range(column):
                z[row] = z[row] - factor[column, row] * z[column]
        for later in range(panel + 2, count):
            terms = [
                spread_lane(state[later], base + column) * z[column] for column in range(GROUP)
            ]
            while len(terms) > 1:
                terms = [terms[at] + terms[at + 1] for at in range(0, len(terms), 2)]
            state[later] = jnp.where(inside, 0.0, state[later]) - terms[0]
    return jnp.concatenate(result, axis=0)


def factor_kernel(
    rounds,
    points_hbm,
    anchors_ref,
    out_ref,
    points_ref,
    table,
    anchor_wide,
    inverse_high,
    inverse_low,
    block_high,
    block_low,
    held,
    load_sem,
    sems,
):
    dims, point_count = points_ref.shape
    total = anchors_ref.shape[1]
    pivot_count = total // rounds
    tile = point_count // rounds
    load = pltpu.make_async_copy(points_hbm, points_ref, load_sem)
    load.start()
    weights = [anchors_ref[dims + axis:dims + axis + 1, :LANES] for axis in range(dims)]
    upright = jnp.transpose(anchors_ref[...])
    for axis in range(dims):
        anchor_wide[axis] = jnp.broadcast_to(upright[:, axis:axis + 1], (total, LANES))
    load.wait()

    def covariance(start, count, targets):
        pieces = []
        for column in range(targets[0].shape[1] // LANES):
            squared = None
            for axis in range(dims):
                offset = anchor_wide[axis, pl.ds(start, count), :] - targets[axis][
                    :, column * LANES:(column + 1) * LANES
                ]
                square = offset * offset
                squared = square if squared is None else squared + square
            pieces.append(jnp.exp2(-squared))
        return jnp.concatenate(pieces, axis=1)

    def one_round(round_index, carry):
        start = pl.multiple_of(round_index * pivot_count, pivot_count)
        here = pl.ds(start, pivot_count)
        span = pl.ds(pl.multiple_of(round_index * tile, tile), tile)
        lane_of = lax.broadcasted_iota(jnp.int32, (pivot_count, total), 1)
        row_of = lax.broadcasted_iota(jnp.int32, (pivot_count, total), 0) + start
        own = covariance(
            start, pivot_count, [anchors_ref[axis:axis + 1, :] for axis in range(dims)]
        )
        own = own + jnp.where(row_of == lane_of, nugget_level, 0.0)
        table[here, :] = jnp.where(lane_of >= start, own, 0.0)

        def subtract(earlier, inner):
            before = pl.multiple_of(earlier * pivot_count, pivot_count)
            seen = pl.ds(before, pivot_count)
            kept = (lane_of < before + pivot_count) | (lane_of >= start)
            table[here, :] = table[here, :] - lax.dot_general(
                table[seen, here],
                jnp.where(kept, table[seen, :], 0.0),
                (((0,), (0,)), ((), ())),
                precision=HIGHEST,
                preferred_element_type=jnp.float32,
            )
            return inner

        lax.fori_loop(0, round_index, subtract, 0)

        targets = [
            points_ref[axis:axis + 1, span]
            * jnp.concatenate([weights[axis]] * (tile // LANES), axis=1)
            for axis in range(dims)
        ]

        def beside(step, steps):
            size = total // steps
            part = slice(step * size, (step + 1) * size)
            values = covariance(step * size, size, targets)
            high = values.astype(jnp.bfloat16)
            block_high[part, span] = high
            block_low[part, span] = (values - high.astype(jnp.float32)).astype(jnp.bfloat16)

        inverse = invert_factor(table[here, here], beside)
        table[here, :] = jnp.dot(
            inverse, table[here, :], precision=HIGHEST, preferred_element_type=jnp.float32
        )
        table[here, here] = inverse
        final = jnp.where(lane_of < start + pivot_count, table[here, :], 0.0)
        high = final.astype(jnp.bfloat16)
        inverse_high[here, :] = high
        inverse_low[here, :] = (final - high.astype(jnp.float32)).astype(jnp.bfloat16)
        return carry

    lax.fori_loop(0, rounds, one_round, 0)

    half = total // 2

    def copy_out(index):
        span = pl.ds(pl.multiple_of(index * tile, tile), tile)
        return pltpu.make_async_copy(held.at[:, span], out_ref.at[:, span], sems.at[index])

    def product(rows, depth, span):
        def multiply(a, b):
            return jnp.dot(
                a[rows, depth], b[depth, span], preferred_element_type=jnp.float32
            )

        return (
            multiply(inverse_high, block_low) + multiply(inverse_low, block_high)
        ) + multiply(inverse_high, block_high)

    def one_tile(index, carry):
        span = pl.ds(pl.multiple_of(index * tile, tile), tile)
        top, bottom = slice(0, half), slice(half, total)
        held[:, span] = product(slice(0, total), top, span)
        held[bottom, span] = held[bottom, span] + product(bottom, bottom, span)
        copy_out(index).start()
        return carry

    lax.fori_loop(0, rounds, one_tile, 0)

    def finish(index, carry):
        copy_out(index).wait()
        return carry

    lax.fori_loop(0, rounds, finish, 0)


def per_device(mesh_shape, points, scales, pivots):
    dims, point_count = points.shape
    rounds, pivot_count = pivots.shape
    total = rounds * pivot_count
    devices = mesh_shape[0] * mesh_shape[1]
    inner = 1
    while inner * inner < devices:
        inner *= 2
    if devices % inner:
        inner = devices
    near, far = inner - 1, devices // inner - 1
    vmem = pl.BlockSpec(memory_space=pltpu.VMEM)
    anywhere = pl.BlockSpec(memory_space=pl.ANY)
    anchors = pl.pallas_call(
        functools.partial(exchange_kernel, mesh_shape, inner),
        out_shape=jax.ShapeDtypeStruct((GROUP, total), jnp.float32),
        in_specs=[anywhere] * 3,
        out_specs=vmem,
        scratch_shapes=[
            pltpu.VMEM((dims, point_count), jnp.float32),
            pltpu.SMEM((dims,), jnp.float32),
            pltpu.VMEM((rounds, pivot_count), jnp.int32),
            pltpu.VMEM((point_count // LANES * GROUP, LANES), jnp.float32),
            pltpu.VMEM((dims, total), jnp.float32),
            pltpu.VMEM((dims, total), jnp.float32),
            pltpu.VMEM((max(near, 1), dims, total), jnp.float32),
            pltpu.VMEM((max(far, 1), dims, total), jnp.float32),
            pltpu.SemaphoreType.DMA((3,)),
            pltpu.SemaphoreType.DMA((max(near, 1),)),
            pltpu.SemaphoreType.DMA((max(near, 1),)),
            pltpu.SemaphoreType.DMA((max(far, 1),)),
            pltpu.SemaphoreType.DMA((max(far, 1),)),
        ],
        compiler_params=pltpu.CompilerParams(
            collective_id=0, has_side_effects=True, vmem_limit_bytes=56 * 2 ** 20
        ),
        name="exchange_anchors",
    )(points, scales, pivots)
    return pl.pallas_call(
        functools.partial(factor_kernel, rounds),
        out_shape=jax.ShapeDtypeStruct((total, point_count), jnp.float32),
        in_specs=[anywhere, vmem],
        out_specs=anywhere,
        scratch_shapes=[
            pltpu.VMEM((dims, point_count), jnp.float32),
            pltpu.VMEM((total, total), jnp.float32),
            pltpu.VMEM((dims, total, LANES), jnp.float32),
            pltpu.VMEM((total, total), jnp.bfloat16),
            pltpu.VMEM((total, total), jnp.bfloat16),
            pltpu.VMEM((total, point_count), jnp.bfloat16),
            pltpu.VMEM((total, point_count), jnp.bfloat16),
            pltpu.VMEM((total, point_count), jnp.float32),
            pltpu.SemaphoreType.DMA,
            pltpu.SemaphoreType.DMA((rounds,)),
        ],
        compiler_params=pltpu.CompilerParams(vmem_limit_bytes=56 * 2 ** 20),
        name="factor_columns",
    )(points, anchors)


def solution(mesh):
    placed = (P(None, ("pts", "rep")), P(), P())
    mesh_shape = (mesh.shape["pts"], mesh.shape["rep"])
    return jax.shard_map(
        functools.partial(per_device, mesh_shape),
        mesh=mesh,
        in_specs=placed,
        out_specs=P(None, ("pts", "rep")),
        check_vma=False,
    )
```

```python
import functools
import math

import jax
import jax.numpy as jnp
from jax import lax
from jax.experimental import pallas as pl
from jax.experimental.pallas import tpu as pltpu
from jax.sharding import PartitionSpec as P

nugget_level = 0.1
HIGHEST = lax.Precision.HIGHEST
LANES = 128
GROUP = 8


def split_three(value):
    high = value.astype(jnp.bfloat16)
    rest = value - high.astype(jnp.float32)
    middle = rest.astype(jnp.bfloat16)
    low = (rest - middle.astype(jnp.float32)).astype(jnp.bfloat16)
    return high, middle, low


def exchange_kernel(
    mesh_shape,
    inner,
    points_hbm,
    scales_hbm,
    pivots_hbm,
    out_ref,
    points_ref,
    scales_ref,
    pivots_ref,
    table,
    mine,
    pair_sum,
    landed_near,
    landed_far,
    load_sems,
    near_send,
    near_recv,
    far_send,
    far_recv,
):
    pts_count, rep_count = mesh_shape
    devices = pts_count * rep_count
    here = lax.axis_index("pts") * rep_count + lax.axis_index("rep")
    dims, point_count = points_ref.shape
    rounds, pivot_count = pivots_ref.shape
    within = lax.rem(here, inner)

    def place(peer):
        return {"pts": peer // rep_count, "rep": lax.rem(peer, rep_count)}

    near = [place(here - within + lax.rem(within + step, inner)) for step in range(1, inner)]
    far = [place(lax.rem(here + step * inner, devices)) for step in range(1, devices // inner)]

    loads = [
        pltpu.make_async_copy(points_hbm, points_ref, load_sems.at[0]),
        pltpu.make_async_copy(pivots_hbm, pivots_ref, load_sems.at[1]),
        pltpu.make_async_copy(scales_hbm, scales_ref, load_sems.at[2]),
    ]
    for load in loads:
        load.start()

    barrier = pltpu.get_barrier_semaphore()
    for target in near + far:
        pl.semaphore_signal(
            barrier, inc=1, device_id=target, device_id_type=pl.DeviceIdType.MESH
        )

    chunks = point_count // LANES
    table[...] = jnp.zeros_like(table)
    for load in loads:
        load.wait()
    for chunk in range(chunks):
        table[chunk * GROUP:chunk * GROUP + dims, :] = points_ref[
            :, chunk * LANES:(chunk + 1) * LANES
        ]
    pieces = split_three(table[...])
    lane_of = lax.broadcasted_iota(jnp.int32, (LANES, pivot_count), 0)
    for round_index in range(rounds):
        local = pivots_ref[round_index:round_index + 1, :] - here * point_count
        owned = (local >= 0) & (local < point_count)
        local = jnp.where(owned, local, 0)
        low = lax.rem(local, LANES)
        high = jnp.where(owned, local // LANES, -1)
        picks = (lane_of == low).astype(jnp.bfloat16)
        found = sum(
            jnp.dot(piece, picks, preferred_element_type=jnp.float32) for piece in pieces
        )
        total = jnp.zeros((GROUP, pivot_count), jnp.float32)
        for chunk in range(chunks):
            total = total + jnp.where(
                high == chunk, found[chunk * GROUP:(chunk + 1) * GROUP, :], 0.0
            )
        mine[:, round_index * pivot_count:(round_index + 1) * pivot_count] = total[:dims]

    pl.semaphore_wait(barrier, len(near) + len(far))

    def exchange(source, landed, targets, send_sems, recv_sems):
        copies = [
            pltpu.make_async_remote_copy(
                src_ref=source,
                dst_ref=landed.at[index],
                send_sem=send_sems.at[index],
                recv_sem=recv_sems.at[index],
                device_id=target,
                device_id_type=pl.DeviceIdType.MESH,
            )
            for index, target in enumerate(targets)
        ]
        for copy in copies:
            copy.start()
        total = source[...]
        for index, copy in enumerate(copies):
            copy.wait_recv()
            total = total + landed[index]
        return total, copies

    total, near_copies = exchange(mine, landed_near, near, near_send, near_recv)
    pair_sum[...] = total
    total, far_copies = exchange(pair_sum, landed_far, far, far_send, far_recv)
    constant = math.sqrt(0.5 * math.log2(math.e))
    out_ref[...] = jnp.zeros_like(out_ref)
    for axis in range(dims):
        weight = constant / jnp.full((1, total.shape[1]), scales_ref[axis], jnp.float32)
        out_ref[axis:axis + 1, :] = total[axis:axis + 1, :] * weight
        out_ref[dims + axis:dims + axis + 1, :] = weight
    for copy in near_copies + far_copies:
        copy.wait_send()


def reciprocal(value):
    return pl.reciprocal(value, approx=True)


def spread_lane(block, lane):
    return jnp.broadcast_to(block[:, lane:lane + 1], block.shape)


def spread_row(block, row):
    return jnp.broadcast_to(block[row:row + 1, :], block.shape)


def invert_factor(block, beside):
    size = block.shape[0]
    count = size // GROUP
    row_of = lax.broadcasted_iota(jnp.int32, (GROUP, size), 0)
    lane_of = lax.broadcasted_iota(jnp.int32, (GROUP, size), 1)
    state = [block[GROUP * index:GROUP * (index + 1), :] for index in range(count)]
    result = []
    for panel in range(count):
        base = GROUP * panel
        beside(panel, count)
        inside = (lane_of >= base) & (lane_of < base + GROUP)
        unit = jnp.where(row_of + base == lane_of, 1.0, 0.0)
        spread = [spread_lane(state[panel], base + column) for column in range(GROUP)]
        s = {
            (i, j): spread_row(spread[j], i) for j in range(GROUP) for i in range(j, GROUP)
        }
        own = jnp.where(inside, unit, state[panel])
        y = [spread_row(own, row) for row in range(GROUP)]
        more = panel + 1 < count
        if more:
            beyond = [
                spread_lane(state[panel + 1], base + column) for column in range(GROUP)
            ]
            follower = jnp.where(inside, 0.0, state[panel + 1])
        inverse = [None] * GROUP
        factor = {}
        z = [None] * GROUP
        for first in range(0, GROUP, 2):
            second = first + 1
            a, b, c = s[first, first], s[second, first], s[second, second]
            over = reciprocal(a * c - b * b)
            inverse[first] = reciprocal(a)
            inverse[second] = a * over
            urgent = {
                (i, j)
                for j in range(second + 1, min(second + 3, GROUP))
                for i in range(j, min(second + 3, GROUP))
            }
            for column in (first, second):
                for i in range(column + 1, GROUP):
                    factor[i, column] = s[i, column] * inverse[column]
                for j in range(column + 1, GROUP):
                    for i in range(j, GROUP):
                        if (i, j) == (second, second):
                            continue
                        if column == second and (i, j) in urgent:
                            change = (s[i, column] * s[j, column]) * a * over
                        else:
                            change = factor[j, column] * s[i, column]
                        s[i, j] = s[i, j] - change
                for i in range(column + 1, GROUP):
                    y[i] = y[i] - factor[i, column] * y[column]
                z[column] = y[column] * inverse[column]
                if more:
                    for k in range(column + 1, GROUP):
                        beyond[k] = beyond[k] - beyond[column] * factor[k, column]
                    follower = follower - beyond[column] * z[column]
        rows, roots = y[0], inverse[0]
        for row in range(1, GROUP):
            rows = jnp.where(row_of == row, y[row], rows)
            roots = jnp.where(row_of == row, inverse[row], roots)
        result.append(jnp.where(lane_of < base + GROUP, rows * jnp.sqrt(roots), 0.0))
        if not more:
            break
        state[panel + 1] = follower
        if panel + 2 == count:
            continue
        for column in reversed(range(GROUP)):
            for row in range(column):
                z[row] = z[row] - factor[column, row] * z[column]
        for later in range(panel + 2, count):
            terms = [
                spread_lane(state[later], base + column) * z[column] for column in range(GROUP)
            ]
            while len(terms) > 1:
                terms = [terms[at] + terms[at + 1] for at in range(0, len(terms), 2)]
            state[later] = jnp.where(inside, 0.0, state[later]) - terms[0]
    return jnp.concatenate(result, axis=0)


def split_two(value):
    high = value.astype(jnp.bfloat16)
    return high, (value - high.astype(jnp.float32)).astype(jnp.bfloat16)


def product(a, b):
    return jnp.dot(
        jnp.concatenate([a[0], a[0], a[1]], axis=1),
        jnp.concatenate([b[0], b[1], b[0]], axis=0),
        preferred_element_type=jnp.float32,
    )


def factor_kernel(
    rounds,
    points_hbm,
    anchors_ref,
    out_ref,
    points_ref,
    table,
    anchor_wide,
    rest_high,
    rest_low,
    done_high,
    done_low,
    held,
    load_sem,
    sems,
):
    dims, point_count = points_ref.shape
    total = anchors_ref.shape[1]
    pivot_count = total // rounds
    chunk = 2 * LANES
    load = pltpu.make_async_copy(points_hbm, points_ref, load_sem)
    load.start()
    weights = [anchors_ref[dims + axis:dims + axis + 1, :LANES] for axis in range(dims)]
    upright = jnp.transpose(anchors_ref[...])
    for axis in range(dims):
        anchor_wide[axis] = jnp.broadcast_to(upright[:, axis:axis + 1], (total, LANES))
    load.wait()

    def covariance(start, targets):
        pieces = []
        for column in range(targets[0].shape[1] // LANES):
            squared = None
            for axis in range(dims):
                offset = anchor_wide[axis, start:start + pivot_count, :] - targets[axis][
                    :, column * LANES:(column + 1) * LANES
                ]
                square = offset * offset
                squared = square if squared is None else squared + square
            pieces.append(jnp.exp2(-squared))
        return jnp.concatenate(pieces, axis=1)

    def solve(round_index, inverse, span):
        rows = slice(round_index * pivot_count, (round_index + 1) * pivot_count)
        slot = round_index % 2
        values = product(inverse, (rest_high[slot, :, span], rest_low[slot, :, span]))
        held[rows, span] = values
        if round_index + 1 < rounds:
            done_high[rows, span], done_low[rows, span] = split_two(values)

    def copy_out(round_index):
        rows = slice(round_index * pivot_count, (round_index + 1) * pivot_count)
        return pltpu.make_async_copy(held.at[rows], out_ref.at[rows], sems.at[round_index])

    inverse_parts = None
    for round_index in range(rounds):
        start = round_index * pivot_count
        end = start + pivot_count
        own = covariance(
            start, [anchors_ref[axis:axis + 1, start:] for axis in range(dims)]
        )
        shape = own.shape
        own = own + jnp.where(
            lax.broadcasted_iota(jnp.int32, shape, 0)
            == lax.broadcasted_iota(jnp.int32, shape, 1),
            nugget_level,
            0.0,
        )
        lower_parts = None
        if round_index:
            lower = jnp.transpose(table[:start, start:end])
            own = own - jnp.dot(
                lower,
                table[:start, start:],
                precision=HIGHEST,
                preferred_element_type=jnp.float32,
            )
            lower_parts = split_two(lower)

        def beside(step, steps):
            width = point_count // steps
            ready = (step + 1) * width
            if ready % chunk:
                return
            for low in range(max(0, ready - max(width, chunk)), ready, chunk):
                span = slice(low, low + chunk)
                if round_index:
                    solve(round_index - 1, inverse_parts, span)
                targets = [
                    points_ref[axis:axis + 1, span]
                    * jnp.concatenate([weights[axis]] * (chunk // LANES), axis=1)
                    for axis in range(dims)
                ]
                rest = covariance(start, targets)
                if round_index:
                    rest = rest - product(
                        lower_parts, (done_high[:start, span], done_low[:start, span])
                    )
                slot = round_index % 2
                rest_high[slot, :, span], rest_low[slot, :, span] = split_two(rest)

        inverse = invert_factor(own[:, :pivot_count], beside)
        if round_index:
            copy_out(round_index - 1).start()
        if round_index + 1 < rounds:
            table[start:end, end:] = jnp.dot(
                inverse,
                own[:, pivot_count:],
                precision=HIGHEST,
                preferred_element_type=jnp.float32,
            )
        inverse_parts = split_two(inverse)

    solve(rounds - 1, inverse_parts, slice(0, point_count))
    copy_out(rounds - 1).start()
    for round_index in range(rounds):
        copy_out(round_index).wait()


def per_device(mesh_shape, points, scales, pivots):
    dims, point_count = points.shape
    rounds, pivot_count = pivots.shape
    total = rounds * pivot_count
    devices = mesh_shape[0] * mesh_shape[1]
    inner = 1
    while inner * inner < devices:
        inner *= 2
    if devices % inner:
        inner = devices
    near, far = inner - 1, devices // inner - 1
    vmem = pl.BlockSpec(memory_space=pltpu.VMEM)
    anywhere = pl.BlockSpec(memory_space=pl.ANY)
    anchors = pl.pallas_call(
        functools.partial(exchange_kernel, mesh_shape, inner),
        out_shape=jax.ShapeDtypeStruct((GROUP, total), jnp.float32),
        in_specs=[anywhere] * 3,
        out_specs=vmem,
        scratch_shapes=[
            pltpu.VMEM((dims, point_count), jnp.float32),
            pltpu.SMEM((dims,), jnp.float32),
            pltpu.VMEM((rounds, pivot_count), jnp.int32),
            pltpu.VMEM((point_count // LANES * GROUP, LANES), jnp.float32),
            pltpu.VMEM((dims, total), jnp.float32),
            pltpu.VMEM((dims, total), jnp.float32),
            pltpu.VMEM((max(near, 1), dims, total), jnp.float32),
            pltpu.VMEM((max(far, 1), dims, total), jnp.float32),
            pltpu.SemaphoreType.DMA((3,)),
            pltpu.SemaphoreType.DMA((max(near, 1),)),
            pltpu.SemaphoreType.DMA((max(near, 1),)),
            pltpu.SemaphoreType.DMA((max(far, 1),)),
            pltpu.SemaphoreType.DMA((max(far, 1),)),
        ],
        compiler_params=pltpu.CompilerParams(
            collective_id=0, has_side_effects=True, vmem_limit_bytes=56 * 2 ** 20
        ),
        name="exchange_anchors",
    )(points, scales, pivots)
    return pl.pallas_call(
        functools.partial(factor_kernel, rounds),
        out_shape=jax.ShapeDtypeStruct((total, point_count), jnp.float32),
        in_specs=[anywhere, vmem],
        out_specs=anywhere,
        scratch_shapes=[
            pltpu.VMEM((dims, point_count), jnp.float32),
            pltpu.VMEM((total, total), jnp.float32),
            pltpu.VMEM((dims, total, LANES), jnp.float32),
            pltpu.VMEM((2, pivot_count, point_count), jnp.bfloat16),
            pltpu.VMEM((2, pivot_count, point_count), jnp.bfloat16),
            pltpu.VMEM((total, point_count), jnp.bfloat16),
            pltpu.VMEM((total, point_count), jnp.bfloat16),
            pltpu.VMEM((total, point_count), jnp.float32),
            pltpu.SemaphoreType.DMA,
            pltpu.SemaphoreType.DMA((rounds,)),
        ],
        compiler_params=pltpu.CompilerParams(vmem_limit_bytes=56 * 2 ** 20),
        name="factor_columns",
    )(points, anchors)


def solution(mesh):
    placed = (P(None, ("pts", "rep")), P(), P())
    mesh_shape = (mesh.shape["pts"], mesh.shape["rep"])
    return jax.shard_map(
        functools.partial(per_device, mesh_shape),
        mesh=mesh,
        in_specs=placed,
        out_specs=P(None, ("pts", "rep")),
        check_vma=False,
    )
```

```python
import functools
import math

import jax
import jax.numpy as jnp
from jax import lax
from jax.experimental import pallas as pl
from jax.experimental.pallas import tpu as pltpu
from jax.sharding import PartitionSpec as P

nugget_level = 0.1
HIGHEST = lax.Precision.HIGHEST
LANES = 128
GROUP = 8


def split_three(value):
    high = value.astype(jnp.bfloat16)
    rest = value - high.astype(jnp.float32)
    middle = rest.astype(jnp.bfloat16)
    low = (rest - middle.astype(jnp.float32)).astype(jnp.bfloat16)
    return high, middle, low


def exchange_kernel(
    mesh_shape,
    inner,
    points_hbm,
    scales_hbm,
    pivots_hbm,
    out_ref,
    scaled_ref,
    points_ref,
    scales_ref,
    pivots_ref,
    table,
    mine,
    pair_sum,
    landed_near,
    landed_far,
    load_sems,
    near_send,
    near_recv,
    far_send,
    far_recv,
):
    pts_count, rep_count = mesh_shape
    devices = pts_count * rep_count
    here = lax.axis_index("pts") * rep_count + lax.axis_index("rep")
    dims, point_count = points_ref.shape
    rounds, pivot_count = pivots_ref.shape
    within = lax.rem(here, inner)

    def place(peer):
        return {"pts": peer // rep_count, "rep": lax.rem(peer, rep_count)}

    near = [place(here - within + lax.rem(within + step, inner)) for step in range(1, inner)]
    far = [place(lax.rem(here + step * inner, devices)) for step in range(1, devices // inner)]

    loads = [
        pltpu.make_async_copy(points_hbm, points_ref, load_sems.at[0]),
        pltpu.make_async_copy(pivots_hbm, pivots_ref, load_sems.at[1]),
        pltpu.make_async_copy(scales_hbm, scales_ref, load_sems.at[2]),
    ]
    for load in loads:
        load.start()

    barrier = pltpu.get_barrier_semaphore()
    for target in near + far:
        pl.semaphore_signal(
            barrier, inc=1, device_id=target, device_id_type=pl.DeviceIdType.MESH
        )

    chunks = point_count // LANES
    table[...] = jnp.zeros_like(table)
    for load in loads:
        load.wait()
    for chunk in range(chunks):
        table[chunk * GROUP:chunk * GROUP + dims, :] = points_ref[
            :, chunk * LANES:(chunk + 1) * LANES
        ]
    pieces = split_three(table[...])
    lane_of = lax.broadcasted_iota(jnp.int32, (LANES, pivot_count), 0)
    for round_index in range(rounds):
        local = pivots_ref[round_index:round_index + 1, :] - here * point_count
        owned = (local >= 0) & (local < point_count)
        local = jnp.where(owned, local, 0)
        low = lax.rem(local, LANES)
        high = jnp.where(owned, local // LANES, -1)
        picks = (lane_of == low).astype(jnp.bfloat16)
        found = sum(
            jnp.dot(piece, picks, preferred_element_type=jnp.float32) for piece in pieces
        )
        total = jnp.zeros((GROUP, pivot_count), jnp.float32)
        for chunk in range(chunks):
            total = total + jnp.where(
                high == chunk, found[chunk * GROUP:(chunk + 1) * GROUP, :], 0.0
            )
        mine[:, round_index * pivot_count:(round_index + 1) * pivot_count] = total[:dims]

    constant = math.sqrt(0.5 * math.log2(math.e))
    weights = [
        constant / jnp.full((1, LANES), scales_ref[axis], jnp.float32) for axis in range(dims)
    ]
    for axis in range(dims):
        scaled_ref[axis:axis + 1, :] = points_ref[axis:axis + 1, :] * jnp.concatenate(
            [weights[axis]] * chunks, axis=1
        )
    pl.semaphore_wait(barrier, len(near) + len(far))

    def exchange(source, landed, targets, send_sems, recv_sems):
        copies = [
            pltpu.make_async_remote_copy(
                src_ref=source,
                dst_ref=landed.at[index],
                send_sem=send_sems.at[index],
                recv_sem=recv_sems.at[index],
                device_id=target,
                device_id_type=pl.DeviceIdType.MESH,
            )
            for index, target in enumerate(targets)
        ]
        for copy in copies:
            copy.start()
        total = source[...]
        for index, copy in enumerate(copies):
            copy.wait_recv()
            total = total + landed[index]
        return total, copies

    total, near_copies = exchange(mine, landed_near, near, near_send, near_recv)
    pair_sum[...] = total
    total, far_copies = exchange(pair_sum, landed_far, far, far_send, far_recv)
    out_ref[...] = jnp.zeros_like(out_ref)
    for axis in range(dims):
        out_ref[axis:axis + 1, :] = total[axis:axis + 1, :] * jnp.concatenate(
            [weights[axis]] * (total.shape[1] // LANES), axis=1
        )
    for copy in near_copies + far_copies:
        copy.wait_send()


def reciprocal(value):
    return pl.reciprocal(value, approx=True)


def spread_lane(block, lane):
    return jnp.broadcast_to(block[:, lane:lane + 1], block.shape)


def spread_row(block, row):
    return jnp.broadcast_to(block[row:row + 1, :], block.shape)


def invert_factor(block, beside):
    size = block.shape[0]
    count = size // GROUP
    row_of = lax.broadcasted_iota(jnp.int32, (GROUP, size), 0)
    lane_of = lax.broadcasted_iota(jnp.int32, (GROUP, size), 1)
    state = [block[GROUP * index:GROUP * (index + 1), :] for index in range(count)]
    result = []
    for panel in range(count):
        base = GROUP * panel
        beside(panel, count)
        inside = (lane_of >= base) & (lane_of < base + GROUP)
        unit = jnp.where(row_of + base == lane_of, 1.0, 0.0)
        spread = [spread_lane(state[panel], base + column) for column in range(GROUP)]
        s = {
            (i, j): spread_row(spread[j], i) for j in range(GROUP) for i in range(j, GROUP)
        }
        own = jnp.where(inside, unit, state[panel])
        y = [spread_row(own, row) for row in range(GROUP)]
        more = panel + 1 < count
        if more:
            beyond = [
                spread_lane(state[panel + 1], base + column) for column in range(GROUP)
            ]
            follower = jnp.where(inside, 0.0, state[panel + 1])
        inverse = [None] * GROUP
        factor = {}
        z = [None] * GROUP
        for first in range(0, GROUP, 2):
            second = first + 1
            a, b, c = s[first, first], s[second, first], s[second, second]
            over = reciprocal(a * c - b * b)
            inverse[first] = reciprocal(a)
            inverse[second] = a * over
            urgent = {
                (i, j)
                for j in range(second + 1, min(second + 3, GROUP))
                for i in range(j, min(second + 3, GROUP))
            }
            for column in (first, second):
                for i in range(column + 1, GROUP):
                    factor[i, column] = s[i, column] * inverse[column]
                for j in range(column + 1, GROUP):
                    for i in range(j, GROUP):
                        if (i, j) == (second, second):
                            continue
                        if column == second and (i, j) in urgent:
                            change = (s[i, column] * s[j, column]) * a * over
                        else:
                            change = factor[j, column] * s[i, column]
                        s[i, j] = s[i, j] - change
                for i in range(column + 1, GROUP):
                    y[i] = y[i] - factor[i, column] * y[column]
                z[column] = y[column] * inverse[column]
                if more:
                    for k in range(column + 1, GROUP):
                        beyond[k] = beyond[k] - beyond[column] * factor[k, column]
                    follower = follower - beyond[column] * z[column]
        rows, roots = y[0], inverse[0]
        for row in range(1, GROUP):
            rows = jnp.where(row_of == row, y[row], rows)
            roots = jnp.where(row_of == row, inverse[row], roots)
        result.append(jnp.where(lane_of < base + GROUP, rows * jnp.sqrt(roots), 0.0))
        if not more:
            break
        state[panel + 1] = follower
        if panel + 2 == count:
            continue
        for column in reversed(range(GROUP)):
            for row in range(column):
                z[row] = z[row] - factor[column, row] * z[column]
        for later in range(panel + 2, count):
            terms = [
                spread_lane(state[later], base + column) * z[column] for column in range(GROUP)
            ]
            while len(terms) > 1:
                terms = [terms[at] + terms[at + 1] for at in range(0, len(terms), 2)]
            state[later] = jnp.where(inside, 0.0, state[later]) - terms[0]
    return jnp.concatenate(result, axis=0)


def split_two(value):
    high = value.astype(jnp.bfloat16)
    return high, (value - high.astype(jnp.float32)).astype(jnp.bfloat16)


def product(a, b):
    return jnp.dot(
        jnp.concatenate([a[0], a[0], a[1]], axis=1),
        jnp.concatenate([b[0], b[1], b[0]], axis=0),
        preferred_element_type=jnp.float32,
    )


def factor_kernel(
    rounds,
    points_ref,
    anchors_ref,
    out_ref,
    table,
    anchor_wide,
    rest_high,
    rest_low,
    done_high,
    done_low,
    held,
    sems,
    last_sems,
):
    dims, point_count = points_ref.shape
    total = anchors_ref.shape[1]
    pivot_count = total // rounds
    chunk = 2 * LANES
    upright = jnp.transpose(anchors_ref[...])
    for axis in range(dims):
        anchor_wide[axis] = jnp.broadcast_to(upright[:, axis:axis + 1], (total, LANES))

    def covariance(start, targets):
        pieces = []
        for column in range(targets[0].shape[1] // LANES):
            squared = None
            for axis in range(dims):
                offset = anchor_wide[axis, start:start + pivot_count, :] - targets[axis][
                    :, column * LANES:(column + 1) * LANES
                ]
                square = offset * offset
                squared = square if squared is None else squared + square
            pieces.append(jnp.exp2(-squared))
        return jnp.concatenate(pieces, axis=1)

    def solve(round_index, inverse, span):
        rows = slice(round_index * pivot_count, (round_index + 1) * pivot_count)
        slot = round_index % 2
        values = product(inverse, (rest_high[slot, :, span], rest_low[slot, :, span]))
        held[rows, span] = values
        if round_index + 1 < rounds:
            done_high[rows, span], done_low[rows, span] = split_two(values)

    def copy_out(round_index):
        rows = slice(round_index * pivot_count, (round_index + 1) * pivot_count)
        return pltpu.make_async_copy(held.at[rows], out_ref.at[rows], sems.at[round_index])

    inverse_parts = None
    for round_index in range(rounds):
        start = round_index * pivot_count
        end = start + pivot_count
        own = covariance(
            start, [anchors_ref[axis:axis + 1, start:] for axis in range(dims)]
        )
        shape = own.shape
        own = own + jnp.where(
            lax.broadcasted_iota(jnp.int32, shape, 0)
            == lax.broadcasted_iota(jnp.int32, shape, 1),
            nugget_level,
            0.0,
        )
        lower_parts = None
        if round_index:
            lower = jnp.transpose(table[:start, start:end])
            own = own - jnp.dot(
                lower,
                table[:start, start:],
                precision=HIGHEST,
                preferred_element_type=jnp.float32,
            )
            lower_parts = split_two(lower)

        def beside(step, steps):
            width = point_count // steps
            ready = (step + 1) * width
            if ready % chunk:
                return
            for low in range(max(0, ready - max(width, chunk)), ready, chunk):
                span = slice(low, low + chunk)
                if round_index:
                    solve(round_index - 1, inverse_parts, span)
                targets = [points_ref[axis:axis + 1, span] for axis in range(dims)]
                rest = covariance(start, targets)
                if round_index:
                    rest = rest - product(
                        lower_parts, (done_high[:start, span], done_low[:start, span])
                    )
                slot = round_index % 2
                rest_high[slot, :, span], rest_low[slot, :, span] = split_two(rest)

        inverse = invert_factor(own[:, :pivot_count], beside)
        if round_index:
            copy_out(round_index - 1).start()
        if round_index + 1 < rounds:
            table[start:end, end:] = jnp.dot(
                inverse,
                own[:, pivot_count:],
                precision=HIGHEST,
                preferred_element_type=jnp.float32,
            )
        inverse_parts = split_two(inverse)

    last_rows = slice(total - pivot_count, total)
    width = point_count // rounds
    last_copies = []
    for piece in range(rounds):
        span = slice(piece * width, (piece + 1) * width)
        solve(rounds - 1, inverse_parts, span)
        last_copies.append(
            pltpu.make_async_copy(
                held.at[last_rows, span], out_ref.at[last_rows, span], last_sems.at[piece]
            )
        )
        last_copies[-1].start()
    for round_index in range(rounds - 1):
        copy_out(round_index).wait()
    for copy in last_copies:
        copy.wait()


def per_device(mesh_shape, points, scales, pivots):
    dims, point_count = points.shape
    rounds, pivot_count = pivots.shape
    total = rounds * pivot_count
    devices = mesh_shape[0] * mesh_shape[1]
    inner = 1
    while inner * inner < devices:
        inner *= 2
    if devices % inner:
        inner = devices
    near, far = inner - 1, devices // inner - 1
    vmem = pl.BlockSpec(memory_space=pltpu.VMEM)
    anywhere = pl.BlockSpec(memory_space=pl.ANY)
    anchors, scaled = pl.pallas_call(
        functools.partial(exchange_kernel, mesh_shape, inner),
        out_shape=[
            jax.ShapeDtypeStruct((GROUP, total), jnp.float32),
            jax.ShapeDtypeStruct((dims, point_count), jnp.float32),
        ],
        in_specs=[anywhere] * 3,
        out_specs=[vmem, vmem],
        scratch_shapes=[
            pltpu.VMEM((dims, point_count), jnp.float32),
            pltpu.SMEM((dims,), jnp.float32),
            pltpu.VMEM((rounds, pivot_count), jnp.int32),
            pltpu.VMEM((point_count // LANES * GROUP, LANES), jnp.float32),
            pltpu.VMEM((dims, total), jnp.float32),
            pltpu.VMEM((dims, total), jnp.float32),
            pltpu.VMEM((max(near, 1), dims, total), jnp.float32),
            pltpu.VMEM((max(far, 1), dims, total), jnp.float32),
            pltpu.SemaphoreType.DMA((3,)),
            pltpu.SemaphoreType.DMA((max(near, 1),)),
            pltpu.SemaphoreType.DMA((max(near, 1),)),
            pltpu.SemaphoreType.DMA((max(far, 1),)),
            pltpu.SemaphoreType.DMA((max(far, 1),)),
        ],
        compiler_params=pltpu.CompilerParams(
            collective_id=0, has_side_effects=True, vmem_limit_bytes=56 * 2 ** 20
        ),
        name="exchange_anchors",
    )(points, scales, pivots)
    return pl.pallas_call(
        functools.partial(factor_kernel, rounds),
        out_shape=jax.ShapeDtypeStruct((total, point_count), jnp.float32),
        in_specs=[vmem, vmem],
        out_specs=anywhere,
        scratch_shapes=[
            pltpu.VMEM((total, total), jnp.float32),
            pltpu.VMEM((dims, total, LANES), jnp.float32),
            pltpu.VMEM((2, pivot_count, point_count), jnp.bfloat16),
            pltpu.VMEM((2, pivot_count, point_count), jnp.bfloat16),
            pltpu.VMEM((total, point_count), jnp.bfloat16),
            pltpu.VMEM((total, point_count), jnp.bfloat16),
            pltpu.VMEM((total, point_count), jnp.float32),
            pltpu.SemaphoreType.DMA((rounds,)),
            pltpu.SemaphoreType.DMA((rounds,)),
        ],
        compiler_params=pltpu.CompilerParams(vmem_limit_bytes=56 * 2 ** 20),
        name="factor_columns",
    )(scaled, anchors)


def solution(mesh):
    placed = (P(None, ("pts", "rep")), P(), P())
    mesh_shape = (mesh.shape["pts"], mesh.shape["rep"])
    return jax.shard_map(
        functools.partial(per_device, mesh_shape),
        mesh=mesh,
        in_specs=placed,
        out_specs=P(None, ("pts", "rep")),
        check_vma=False,
    )
```
